32 devices in a mesh: groups: 2 (over y), node: 4 (over x, core), local: 4 (over z).
Axes of the slice: x: 2, y: 2, z: 4, core: 2. Of those that a mesh axis runs over, the one named last changes fastest.
Arguments:
- tokens: bfloat16 [256, 3584], P(('groups', 'node', 'local')), parts along dimension 0, may hold values from -6 to 6
- expert_ids: int32 [256, 4], P(('groups', 'node', 'local')), parts along dimension 0, may hold values from 0 to 3, all different within a row; in each aligned block of 8 rows (0 to 7, 8 to 15, ...) at most 8 rows name the same one
- gate_values: float32 [256, 4], P(('groups', 'node', 'local')), parts along dimension 0, may hold values from 0.05 to 1
- shared_gate: bfloat16 [3584, 1024], P(None, 'local'), may hold values from -0.09375 to 0.09375
- shared_up: bfloat16 [3584, 1024], P(None, 'local'), may hold values from -0.09375 to 0.09375
- shared_down: bfloat16 [1024, 3584], P('local'), may hold values from -0.1875 to 0.1875
- expert_gate: bfloat16 [16, 3584, 256], P(('node', 'local')), may hold values from -0.09375 to 0.09375
- expert_up: bfloat16 [16, 3584, 256], P(('node', 'local')), may hold values from -0.09375 to 0.09375
- expert_down: bfloat16 [16, 256, 3584], P(('node', 'local')), may hold values from -0.1875 to 0.1875
Outputs:
- mixed: bfloat16 [256, 3584], P(('groups', 'node', 'local')), parts along dimension 0
The draws below stay inside these ranges and needn't reach their ends.
There are 2 independent parts, one for each index of `groups`. The reference program is written for one: setup_inputs(seed, part) draws one part's arguments, and reference() takes and returns one part's arrays. A program takes and returns all parts, laid end to end along the dimension named above; an argument that names none is the same for every part. Nothing has to cross between parts.
Inputs may be any that keep to these rules, and one draw needn't show every extreme that they name: `expert_ids`: each row names 4 different experts. Among the 8 rows of one device (aligned blocks), no expert is named by more than 8 rows.
All inputs are finite; a program needn't handle non-finite values.
Results may differ from the reference program's by a relative error of at most 0.0055.
Values may be sent and summed in bfloat16 or wider, within the bound.
A program may use at most 64 MiB of HBM per device.

```python
import math
import jax
import jax.numpy as jnp
import numpy as np
from jax import lax

D = 3584
F = 1024
SF = 1024
SHARDS = 4
TOK_DEV = 8
F_SHARD = 256
EXPERTS = 4
TOPK = 4
CAP = 8
TOKENS = 128
N_NODE = 4
N_LOCAL = 4


def block_levels(own_key, dims, shards, low, top_value):
    factor_of = 1.0
    for dim, shards_of in shards:
        steps = jax.random.uniform(jax.random.fold_in(jax.random.fold_in(own_key, 6), dim), (shards_of,), jnp.float32, low / len(shards), top_value / len(shards))
        factor_of = factor_of * jnp.repeat(jnp.exp(steps), dims[dim] // shards_of).reshape((-1,) + (1,) * (len(dims) - 1 - dim))
    return factor_of


def deal_out(own_key, own, number, rows, count, top, bound, lean):
    order = jax.random.permutation(own_key, count)
    crowded, usual = load_shares(count, rows * top, bound, lean, True), load_shares(count, rows * top, bound, lean, False)
    places = jnp.arange(count)

    def named(tallies, offset_by):
        used = int((tallies > 0).sum())
        fixed = max(1, used // 4)
        passed = fixed + (places - fixed + offset_by * (used - fixed)) % max(1, count - fixed)
        return jnp.zeros((count,), jnp.int32).at[order[jnp.where(places < fixed, places, passed)]].set(jnp.asarray(tallies, jnp.int32))

    tallies = jnp.where(number % 4 == 0, named(crowded, number // 4), named(usual, number - number // 4 - 1))
    mixed = jax.random.permutation(jax.random.fold_in(own, 3), count)
    giver, sink = mixed[0:count // 2 * 2:2], mixed[1:count // 2 * 2:2]
    room = jnp.minimum(tallies[giver] - 1, bound - tallies[sink]) // 2
    room = jnp.where((giver == order[0]) | (sink == order[0]) | (tallies[sink] == 0), 0, jnp.maximum(room, 0))
    passed = jax.random.randint(jax.random.fold_in(own, 4), (count // 2,), 0, 1 << 20) % (room + 1)
    tallies = tallies.at[giver].add(-passed).at[sink].add(passed)
    members = jnp.searchsorted(jnp.cumsum(tallies), jnp.arange(rows * top), side="right").astype(jnp.int32)
    listing = members.reshape(top, rows).T
    listing = listing[jax.random.permutation(jax.random.fold_in(own, 1), rows)]
    offset_by = jax.random.randint(jax.random.fold_in(own, 2), (rows, 1), 0, top)
    return jnp.take_along_axis(listing, (jnp.arange(top)[None, :] + offset_by) % top, axis=1)


def load_shares(count, total, limit, skew, full):
    loads = [(1 << 20) // math.isqrt(rank ** skew) + 1 for rank in range(1, count + 1)]
    largest = limit if full else min(limit, max(-(-total // count), total * loads[0] // sum(loads)))
    least = 1 if total - largest >= count - 1 else 0
    counts, spare = [largest] + [least] * (count - 1), total - largest - least * (count - 1)
    while spare > 0:
        free = [i for i in range(1, count) if counts[i] < largest] or [i for i in range(1, count) if counts[i] < limit]
        mass, left = sum([loads[i] for i in free]), spare
        for i in free:
            extra = min(limit - counts[i], max(1, left * loads[i] // mass), spare)
            counts[i] = counts[i] + extra
            spare = spare - extra
    return np.array(counts)


def gaussian(stream_key, dims, spread, reach, pieces=(), kind=jnp.bfloat16):
    array = jax.random.normal(stream_key, dims, jnp.float32) * spread
    if len(pieces) > 0:
        array = block_levels(stream_key, dims, pieces, -0.22, 0.18) * array
    return jnp.clip(array, min=-reach, max=reach).astype(kind)


def setup_inputs(seed: int = 0, part: int = 0) -> dict:
    seeds = jax.random.split(jax.random.key(seed), 10)
    part_splits = jax.random.split(jax.random.fold_in(seeds[9], part), 10)
    tokens = gaussian(part_splits[0], (TOKENS, D), 1.0, 6.0, ((0, 16),))
    expert_ids_keys = jax.random.split(jax.random.fold_in(part_splits[1], 1), TOKENS // TOK_DEV)
    expert_ids_turns = jax.random.permutation(jax.random.fold_in(part_splits[1], 3), TOKENS // TOK_DEV)
    expert_ids = jax.vmap(lambda own, number: deal_out(jax.random.fold_in(part_splits[1], 2), own, number, TOK_DEV, EXPERTS, TOPK, CAP, 1))(expert_ids_keys, expert_ids_turns).reshape((TOKENS, TOPK))
    gate_values = jnp.clip(0.05 + 0.95 * jax.random.uniform(part_splits[2], (TOKENS, TOPK), jnp.float32) ** block_levels(part_splits[2], (TOKENS, TOPK), ((0, 16),), -0.2, 0.2), 0.05, 1.0)
    shared_gate = gaussian(seeds[3], (D, SF), D ** -0.5, 0.09375, ((1, 4),))
    shared_up = gaussian(seeds[4], (D, SF), D ** -0.5, 0.09375, ((1, 4),))
    shared_down = gaussian(seeds[5], (SF, D), SF ** -0.5, 0.1875, ((0, 4),))
    expert_gate = gaussian(seeds[6], (EXPERTS * SHARDS, D, F_SHARD), D ** -0.5, 0.09375, ((0, 16),))
    expert_up = gaussian(seeds[7], (EXPERTS * SHARDS, D, F_SHARD), D ** -0.5, 0.09375, ((0, 16),))
    expert_down = gaussian(seeds[8], (EXPERTS * SHARDS, F_SHARD, D), F ** -0.5, 0.1875, ((0, 16),))
    return dict(tokens=tokens, expert_ids=expert_ids, gate_values=gate_values, shared_gate=shared_gate, shared_up=shared_up, shared_down=shared_down, expert_gate=expert_gate, expert_up=expert_up, expert_down=expert_down)


def run_block(rows, w_gate, w_up, w_down):
    gate_part = jnp.dot(rows, w_gate, preferred_element_type=jnp.float32)
    up_part = jnp.dot(rows, w_up, preferred_element_type=jnp.float32)
    hidden = (jax.nn.silu(gate_part) * up_part).astype(jnp.bfloat16)
    return jnp.dot(hidden, w_down, preferred_element_type=jnp.float32)


def reference(tokens, expert_ids, gate_values, shared_gate, shared_up, shared_down, expert_gate, expert_up, expert_down):
    device_total = N_NODE * N_LOCAL
    shared_out = run_block(tokens, shared_gate, shared_up, shared_down)
    id_table = expert_ids.reshape(device_total, TOK_DEV, TOPK)
    value_table = gate_values.reshape(device_total, TOK_DEV, TOPK)
    expert_iota = jnp.arange(EXPERTS, dtype=jnp.int32)
    chosen = id_table[..., None] == expert_iota
    onehot = jnp.any(chosen, axis=2).astype(jnp.float32)
    weight_table = jnp.sum(jnp.where(chosen, value_table[..., None], jnp.float32(0.0)), axis=2)
    position = jnp.cumsum(onehot, axis=1) - onehot
    slot_iota = jnp.arange(CAP).astype(jnp.float32)
    token_rows = tokens.reshape(device_total, TOK_DEV, D).astype(jnp.float32)

    def one_expert(total, index):
        picker = onehot[:, :, index][..., None] * (position[:, :, index][..., None] == slot_iota).astype(jnp.float32)
        gathered = jnp.einsum("ntc,ntd->ncd", picker, token_rows, precision=lax.Precision.HIGHEST)
        gathered = gathered.astype(jnp.bfloat16).reshape(device_total * CAP, D)
        result = jnp.zeros((device_total * CAP, D), jnp.float32)
        for shard in range(SHARDS):
            entry = index * SHARDS + shard
            piece = run_block(gathered, expert_gate[entry], expert_up[entry], expert_down[entry])
            piece = lax.optimization_barrier(piece.astype(jnp.bfloat16)).astype(jnp.float32)
            result = result + piece
        result = result.reshape(device_total, CAP, D)
        scaled = picker * weight_table[:, :, index][..., None]
        return total + jnp.einsum("ntc,ncd->ntd", scaled, result, precision=lax.Precision.HIGHEST), None

    start_total = jnp.zeros((device_total, TOK_DEV, D), jnp.float32)
    routed, unused = lax.scan(one_expert, start_total, jnp.arange(EXPERTS, dtype=jnp.int32))
    return (shared_out + routed.reshape(TOKENS, D)).astype(jnp.bfloat16)
```

```python
import functools

import jax
import jax.numpy as jnp
from jax import lax
from jax.experimental import pallas as pl
from jax.experimental.pallas import tpu as pltpu
from jax.sharding import PartitionSpec as P

SHARDS = 4
MESH = pl.DeviceIdType.MESH


def run_block(rows, w_gate, w_up, w_down):
    gate_part = jnp.dot(rows, w_gate, preferred_element_type=jnp.float32)
    up_part = jnp.dot(rows, w_up, preferred_element_type=jnp.float32)
    hidden = (jax.nn.silu(gate_part) * up_part).astype(jnp.bfloat16)
    return jnp.dot(hidden, w_down, preferred_element_type=jnp.float32)


def sparse_shards(
    tokens,
    expert_ids,
    gate_values,
    shared_gate,
    shared_up,
    shared_down,
    expert_gate,
    expert_up,
    expert_down,
):
    tok_dev, model_width = tokens.shape
    top_count = expert_ids.shape[1]
    node_count = lax.axis_size("node")
    local_count = lax.axis_size("local")
    expert_count = node_count * local_count // SHARDS
    capacity = min(tok_dev, max(2, 3 * tok_dev * top_count // (2 * expert_count)))
    shared_terms = run_block(
        lax.all_gather(tokens, "local", axis=0, tiled=True), shared_gate, shared_up, shared_down
    )
    shared_out = lax.psum_scatter(shared_terms, "local", scatter_dimension=0, tiled=True)
    chosen = expert_ids[:, :, None] == jnp.arange(expert_count, dtype=jnp.int32)
    onehot = jnp.any(chosen, axis=1).astype(jnp.float32)
    weight_table = jnp.sum(jnp.where(chosen, gate_values[:, :, None], jnp.float32(0.0)), axis=1)
    position = jnp.cumsum(onehot, axis=0) - onehot
    slot_iota = jnp.arange(capacity).astype(jnp.float32)
    picker = onehot[:, :, None] * (position[:, :, None] == slot_iota).astype(jnp.float32)
    slot_rows = jnp.einsum(
        "tec,td->ecd", picker.astype(jnp.bfloat16), tokens, preferred_element_type=jnp.float32
    ).astype(jnp.bfloat16)
    outgoing = jnp.repeat(slot_rows, SHARDS, axis=0)
    row_block = lax.all_to_all(outgoing, ("node", "local"), split_axis=0, concat_axis=0, tiled=True)
    leading = row_block.shape[:-1]
    flat_rows = row_block.reshape(-1, model_width)
    result = run_block(flat_rows, expert_gate[0], expert_up[0], expert_down[0])
    partial_out = result.astype(jnp.bfloat16).reshape(leading + (model_width,))
    returned = lax.all_to_all(
        partial_out, ("node", "local"), split_axis=0, concat_axis=0, tiled=True
    )
    expert_result = jnp.sum(
        returned.astype(jnp.float32).reshape(expert_count, SHARDS, capacity, model_width), axis=1
    )
    scaled = picker * weight_table[:, :, None]
    routed = jnp.einsum("tec,ecd->td", scaled, expert_result, precision=lax.Precision.HIGHEST)
    return (shared_out + routed).astype(jnp.bfloat16)


def flip(value, bits):
    bit = 1
    while bit <= bits:
        if bits & bit:
            value = value + bit - 2 * bit * ((value // bit) % 2)
        bit *= 2
    return value


def is_power(n):
    return n & (n - 1) == 0


def dense_kernel(
    dims,
    tok_ref, ids_ref, val_ref, sg_ref, su_ref, sd_ref, eg_ref, eu_ref, ed_ref,
    out_ref,
    rows, sg, su, sd, eg, eu, ed,
    keep, sib_out, sib_in, x_out, x_in, z_out, z_in,
    load_sem, send_sem, recv_sem,
):
    nodes, locals_, width, experts = dims
    tok = tok_ref.shape[0]
    node, local = lax.axis_index("node"), lax.axis_index("local")
    evens = range(0, nodes, 2)
    far = range(2, nodes, 2)
    order = list(range(locals_ - 1, 0, -1))

    count = iter(range(1 << 16))
    id_z = {k: next(count) for k in order}
    id_x = {(r, k): next(count) for r in far for k in range(locals_)}
    id_s = {(r, k): next(count) for r in evens for k in range(locals_)}
    id_rs = {(r, k): next(count) for r in evens for k in range(locals_)}
    id_rx = {(r, k): next(count) for r in far for k in range(locals_)}
    id_rz = {k: next(count) for k in order}

    loads = []
    for i, (src, dst) in enumerate((
        (tok_ref, rows.at[0, 0, :, pl.ds(0, width)]),
        (eg_ref.at[0], eg), (eu_ref.at[0], eu), (ed_ref.at[0], ed),
        (sg_ref, sg), (su_ref, su), (sd_ref, sd),
    )):
        loads.append(pltpu.make_async_copy(src, dst, load_sem.at[i]))
        loads[-1].start()

    def at_local(k):
        return {"local": flip(local, k)}

    def at_node(r):
        return {"node": flip(node, r)}

    partners = [at_local(k) for k in order] + [at_node(r) for r in far] + [at_node(1)]
    barrier = pltpu.get_barrier_semaphore()
    for where in partners:
        pl.semaphore_signal(barrier, inc=1, device_id=where, device_id_type=MESH)

    lane = lax.broadcasted_iota(jnp.int32, (tok, 128), 1)
    lane_expert = lax.rem(lane, experts)
    weight = jnp.zeros((tok, 128), jnp.float32)
    for k in range(ids_ref.shape[1]):
        weight = weight + jnp.where(
            ids_ref[:, k:k + 1] == lane_expert, val_ref[:, k:k + 1], jnp.float32(0.0)
        )
    high = weight.astype(jnp.bfloat16).astype(jnp.float32)
    middle = (weight - high).astype(jnp.bfloat16).astype(jnp.float32)
    low = weight - high - middle
    terms = jnp.where(
        lane < experts, high,
        jnp.where(lane < 2 * experts, middle, jnp.where(lane < 3 * experts, low, 0.0)),
    )
    rows[0, 0, :, width:width + 128] = terms.astype(jnp.bfloat16)
    loads[0].wait()
    pl.semaphore_wait(barrier, len(partners))

    started = []

    def send(src, dst, number, where):
        copy = pltpu.make_async_remote_copy(
            src_ref=src, dst_ref=dst,
            send_sem=send_sem.at[number], recv_sem=recv_sem.at[number],
            device_id=where, device_id_type=MESH,
        )
        copy.start()
        started.append(copy)
        return copy

    along_z, along_x, to_core = {}, {}, {}
    for k in order:
        along_z[k] = send(rows.at[0, 0], rows.at[0, k], id_z[k], at_local(k))

    def pass_on(k):
        for r in far:
            along_x[r, k] = send(rows.at[0, k], rows.at[r, k], id_x[r, k], at_node(r))
        to_core[0, k] = send(rows.at[0, k], rows.at[1, k], id_s[0, k], at_node(1))

    arrival = list(range(locals_))
    pass_on(0)
    for k in arrival[1:]:
        along_z[k].wait_recv()
        pass_on(k)

    own_expert = (node * locals_ + local) // SHARDS

    def block(x, w_gate, w_up, w_down):
        g = jnp.dot(x, w_gate[...], preferred_element_type=jnp.float32)
        u = jnp.dot(x, w_up[...], preferred_element_type=jnp.float32)
        h = (g / (1.0 + jnp.exp(-g)) * u).astype(jnp.bfloat16)
        return jnp.dot(h, w_down[...], preferred_element_type=jnp.float32)

    def partial(r):
        held = rows[r].astype(jnp.float32).reshape(locals_ * tok, width + 128)
        x = held[:, :width].astype(jnp.bfloat16)
        tail = held[:, width:]
        lanes = lax.broadcasted_iota(jnp.int32, tail.shape, 1)
        mine = (lax.rem(lanes, experts) == own_expert) & (lanes < 3 * experts)
        factor = jnp.sum(jnp.where(mine, tail, 0.0), axis=1, keepdims=True)
        y = block(x, eg, eu, ed) * factor
        if r == 0:
            y = y + block(x, sg, su, sd)
        return y.reshape(locals_, tok, width)

    core_sums = {}

    def do_chunk(r):
        y = partial(r)
        if r % 2:
            sib_out[r // 2] = y.astype(jnp.bfloat16)
            for k in order + [0]:
                core_sums[r - 1, k] = send(
                    sib_out.at[r // 2, k], sib_in.at[r // 2, k], id_rs[r - 1, k], at_node(1)
                )
        else:
            keep[r // 2] = y

    for load in loads[1:]:
        load.wait()
    do_chunk(0)
    for r in far:
        for k in arrival:
            along_x[r, k].wait_recv()
            to_core[r, k] = send(rows.at[r, k], rows.at[r + 1, k], id_s[r, k], at_node(1))
    for k in arrival:
        to_core[0, k].wait_recv()
    do_chunk(1)
    for r in far:
        do_chunk(r)
        for k in arrival:
            to_core[r, k].wait_recv()
        do_chunk(r + 1)

    x_sums, z_sums = {}, {}
    for r in far:
        for k in order + [0]:
            core_sums[r, k].wait_recv()
            x_out[r // 2 - 1, k] = (
                keep[r // 2, k] + sib_in[r // 2, k].astype(jnp.float32)
            ).astype(jnp.bfloat16)
            x_sums[r, k] = send(
                x_out.at[r // 2 - 1, k], x_in.at[r // 2 - 1, k], id_rx[r, k], at_node(r)
            )
    for k in order + [0]:
        core_sums[0, k].wait_recv()
        total = keep[0, k] + sib_in[0, k].astype(jnp.float32)
        for r in far:
            x_sums[r, k].wait_recv()
            total = total + x_in[r // 2 - 1, k].astype(jnp.float32)
        if k:
            z_out[k] = total.astype(jnp.bfloat16)
            z_sums[k] = send(z_out.at[k], z_in.at[k], id_rz[k], at_local(k))
    for k in reversed(order):
        z_sums[k].wait_recv()
        total = total + z_in[k].astype(jnp.float32)
    out_ref[...] = total.astype(jnp.bfloat16)

    for copy in started:
        copy.wait_send()


def dense_shards(*args):
    tokens, expert_ids = args[0], args[1]
    tok, width = tokens.shape
    hidden, shared_hidden = args[6].shape[2], args[3].shape[1]
    nodes, locals_ = lax.axis_size("node"), lax.axis_size("local")
    experts = nodes * locals_ // SHARDS
    pairs = nodes // 2
    copies = (locals_ - 1) * 2 + (pairs - 1) * locals_ * 2 + pairs * locals_ * 2
    bf16, f32 = jnp.bfloat16, jnp.float32
    any_spec, vmem_spec = pl.BlockSpec(memory_space=pl.ANY), pl.BlockSpec(memory_space=pltpu.VMEM)
    return pl.pallas_call(
        functools.partial(dense_kernel, (nodes, locals_, width, experts)),
        out_shape=jax.ShapeDtypeStruct((tok, width), bf16),
        in_specs=[any_spec, vmem_spec, vmem_spec] + [any_spec] * 6,
        out_specs=vmem_spec,
        scratch_shapes=[
            pltpu.VMEM((nodes, locals_, tok, width + 128), bf16),
            pltpu.VMEM((width, shared_hidden), bf16),
            pltpu.VMEM((width, shared_hidden), bf16),
            pltpu.VMEM((shared_hidden, width), bf16),
            pltpu.VMEM((width, hidden), bf16),
            pltpu.VMEM((width, hidden), bf16),
            pltpu.VMEM((hidden, width), bf16),
            pltpu.VMEM((pairs, locals_, tok, width), f32),
            pltpu.VMEM((pairs, locals_, tok, width), bf16),
            pltpu.VMEM((pairs, locals_, tok, width), bf16),
            pltpu.VMEM((pairs - 1, locals_, tok, width), bf16),
            pltpu.VMEM((pairs - 1, locals_, tok, width), bf16),
            pltpu.VMEM((locals_, tok, width), bf16),
            pltpu.VMEM((locals_, tok, width), bf16),
            pltpu.SemaphoreType.DMA((7,)),
            pltpu.SemaphoreType.DMA((copies,)),
            pltpu.SemaphoreType.DMA((copies,)),
        ],
        compiler_params=pltpu.CompilerParams(
            collective_id=0, has_side_effects=True, vmem_limit_bytes=48 << 20
        ),
        cost_estimate=pl.CostEstimate(
            flops=6 * tok * nodes * locals_ * width * hidden,
            bytes_accessed=2 * 3 * width * (hidden + shared_hidden),
            transcendentals=0,
        ),
    )(*args)


def shards(*args):
    expert_ids = args[1]
    nodes, locals_ = lax.axis_size("node"), lax.axis_size("local")
    experts = nodes * locals_ // SHARDS
    every_expert = expert_ids.shape[1] == experts and 3 * experts <= 128
    if every_expert and nodes >= 4 and is_power(nodes) and is_power(locals_):
        return dense_shards(*args)
    return sparse_shards(*args)


def solution(mesh):
    return jax.shard_map(
        shards,
        mesh=mesh,
        in_specs=(
            P(("groups", "node", "local"), None),
            P(("groups", "node", "local"), None),
            P(("groups", "node", "local"), None),
            P(None, "local"),
            P(None, "local"),
            P("local", None),
            P(("node", "local"), None, None),
            P(("node", "local"), None, None),
            P(("node", "local"), None, None),
        ),
        out_specs=P(("groups", "node", "local"), None),
        check_vma=False,
    )
```

```python
import functools

import jax
import jax.numpy as jnp
from jax import lax
from jax.experimental import pallas as pl
from jax.experimental.pallas import tpu as pltpu
from jax.sharding import PartitionSpec as P

SHARDS = 4
MESH = pl.DeviceIdType.MESH


def run_block(rows, w_gate, w_up, w_down):
    gate_part = jnp.dot(rows, w_gate, preferred_element_type=jnp.float32)
    up_part = jnp.dot(rows, w_up, preferred_element_type=jnp.float32)
    hidden = (jax.nn.silu(gate_part) * up_part).astype(jnp.bfloat16)
    return jnp.dot(hidden, w_down, preferred_element_type=jnp.float32)


def sparse_shards(
    tokens,
    expert_ids,
    gate_values,
    shared_gate,
    shared_up,
    shared_down,
    expert_gate,
    expert_up,
    expert_down,
):
    tok_dev, model_width = tokens.shape
    top_count = expert_ids.shape[1]
    node_count = lax.axis_size("node")
    local_count = lax.axis_size("local")
    expert_count = node_count * local_count // SHARDS
    capacity = min(tok_dev, max(2, 3 * tok_dev * top_count // (2 * expert_count)))
    shared_terms = run_block(
        lax.all_gather(tokens, "local", axis=0, tiled=True), shared_gate, shared_up, shared_down
    )
    shared_out = lax.psum_scatter(shared_terms, "local", scatter_dimension=0, tiled=True)
    chosen = expert_ids[:, :, None] == jnp.arange(expert_count, dtype=jnp.int32)
    onehot = jnp.any(chosen, axis=1).astype(jnp.float32)
    weight_table = jnp.sum(jnp.where(chosen, gate_values[:, :, None], jnp.float32(0.0)), axis=1)
    position = jnp.cumsum(onehot, axis=0) - onehot
    slot_iota = jnp.arange(capacity).astype(jnp.float32)
    picker = onehot[:, :, None] * (position[:, :, None] == slot_iota).astype(jnp.float32)
    slot_rows = jnp.einsum(
        "tec,td->ecd", picker.astype(jnp.bfloat16), tokens, preferred_element_type=jnp.float32
    ).astype(jnp.bfloat16)
    outgoing = jnp.repeat(slot_rows, SHARDS, axis=0)
    row_block = lax.all_to_all(outgoing, ("node", "local"), split_axis=0, concat_axis=0, tiled=True)
    leading = row_block.shape[:-1]
    flat_rows = row_block.reshape(-1, model_width)
    result = run_block(flat_rows, expert_gate[0], expert_up[0], expert_down[0])
    partial_out = result.astype(jnp.bfloat16).reshape(leading + (model_width,))
    returned = lax.all_to_all(
        partial_out, ("node", "local"), split_axis=0, concat_axis=0, tiled=True
    )
    expert_result = jnp.sum(
        returned.astype(jnp.float32).reshape(expert_count, SHARDS, capacity, model_width), axis=1
    )
    scaled = picker * weight_table[:, :, None]
    routed = jnp.einsum("tec,ecd->td", scaled, expert_result, precision=lax.Precision.HIGHEST)
    return (shared_out + routed).astype(jnp.bfloat16)


def flip(value, bits):
    bit = 1
    while bit <= bits:
        if bits & bit:
            value = value + bit - 2 * bit * ((value // bit) % 2)
        bit *= 2
    return value


def is_power(n):
    return n & (n - 1) == 0


def dense_kernel(
    dims,
    tok_ref, ids_ref, val_ref, sg_ref, su_ref, sd_ref, eg_ref, eu_ref, ed_ref,
    out_ref,
    rows, sg, su, sd, eg, eu, ed,
    keep, sib_out, sib_in, x_out, x_in, z_out, z_in,
    load_sem, send_sem, recv_sem,
):
    nodes, locals_, width, experts = dims
    tok = tok_ref.shape[0]
    node, local = lax.axis_index("node"), lax.axis_index("local")
    evens = range(0, nodes, 2)
    far = range(2, nodes, 2)
    order = list(range(locals_ - 1, 0, -1))

    count = iter(range(1 << 16))
    id_z = {k: next(count) for k in order}
    id_x = {(r, k): next(count) for r in far for k in range(locals_)}
    id_s = {(r, k): next(count) for r in evens for k in range(locals_)}
    id_rs = {(r, k): next(count) for r in evens for k in range(locals_)}
    id_rx = {(r, k): next(count) for r in far for k in range(locals_)}
    id_rz = {k: next(count) for k in order}

    loads = []
    for i, (src, dst) in enumerate((
        (tok_ref, rows.at[0, 0, :, pl.ds(0, width)]),
        (eg_ref.at[0], eg), (eu_ref.at[0], eu), (ed_ref.at[0], ed),
        (sg_ref, sg), (su_ref, su), (sd_ref, sd),
    )):
        loads.append(pltpu.make_async_copy(src, dst, load_sem.at[i]))
        loads[-1].start()

    def at_local(k):
        return {"local": flip(local, k)}

    def at_node(r):
        return {"node": flip(node, r)}

    partners = [at_local(k) for k in order] + [at_node(r) for r in far] + [at_node(1)]
    barrier = pltpu.get_barrier_semaphore()
    for where in partners:
        pl.semaphore_signal(barrier, inc=1, device_id=where, device_id_type=MESH)

    lane = lax.broadcasted_iota(jnp.int32, (tok, 128), 1)
    lane_expert = lax.rem(lane, experts)
    across = lax.broadcasted_iota(jnp.int32, (tok, tok), 1)
    diagonal = lax.broadcasted_iota(jnp.int32, (tok, tok), 0) == across

    def column(line):
        return jnp.sum(jnp.where(diagonal, line, 0.0), axis=1, keepdims=True)

    lane_expert = lane_expert.astype(jnp.float32)
    weight = jnp.zeros((tok, 128), jnp.float32)
    for k in range(ids_ref.shape[0]):
        name = column(ids_ref[k:k + 1, :].astype(jnp.float32))
        weight = weight + jnp.where(name == lane_expert, column(val_ref[k:k + 1, :]), 0.0)
    high = weight.astype(jnp.bfloat16).astype(jnp.float32)
    middle = (weight - high).astype(jnp.bfloat16).astype(jnp.float32)
    low = weight - high - middle
    terms = jnp.where(
        lane < experts, high,
        jnp.where(lane < 2 * experts, middle, jnp.where(lane < 3 * experts, low, 0.0)),
    )
    rows[0, 0, :, width:width + 128] = terms.astype(jnp.bfloat16)
    loads[0].wait()
    pl.semaphore_wait(barrier, len(partners))

    started = []

    def send(src, dst, number, where):
        copy = pltpu.make_async_remote_copy(
            src_ref=src, dst_ref=dst,
            send_sem=send_sem.at[number], recv_sem=recv_sem.at[number],
            device_id=where, device_id_type=MESH,
        )
        copy.start()
        started.append(copy)
        return copy

    along_z, along_x, to_core = {}, {}, {}
    for k in order:
        along_z[k] = send(rows.at[0, 0], rows.at[0, k], id_z[k], at_local(k))

    def pass_on(k):
        for r in far:
            along_x[r, k] = send(rows.at[0, k], rows.at[r, k], id_x[r, k], at_node(r))
        to_core[0, k] = send(rows.at[0, k], rows.at[1, k], id_s[0, k], at_node(1))

    arrival = list(range(locals_))
    pass_on(0)
    for k in arrival[1:]:
        along_z[k].wait_recv()
        pass_on(k)

    own_expert = (node * locals_ + local) // SHARDS

    def block(x, w_gate, w_up, w_down):
        g = jnp.dot(x, w_gate[...], preferred_element_type=jnp.float32)
        u = jnp.dot(x, w_up[...], preferred_element_type=jnp.float32)
        h = (g / (1.0 + jnp.exp(-g)) * u).astype(jnp.bfloat16)
        return jnp.dot(h, w_down[...], preferred_element_type=jnp.float32)

    def partial(r):
        held = rows[r].astype(jnp.float32).reshape(locals_ * tok, width + 128)
        x = held[:, :width].astype(jnp.bfloat16)
        tail = held[:, width:]
        lanes = lax.broadcasted_iota(jnp.int32, tail.shape, 1)
        mine = (lax.rem(lanes, experts) == own_expert) & (lanes < 3 * experts)
        factor = jnp.sum(jnp.where(mine, tail, 0.0), axis=1, keepdims=True)
        y = block(x, eg, eu, ed) * factor
        if r == 0:
            y = y + block(x, sg, su, sd)
        return y.reshape(locals_, tok, width)

    core_sums = {}

    def do_chunk(r):
        y = partial(r)
        if r % 2:
            sib_out[r // 2] = y.astype(jnp.bfloat16)
            for k in order + [0]:
                core_sums[r - 1, k] = send(
                    sib_out.at[r // 2, k], sib_in.at[r // 2, k], id_rs[r - 1, k], at_node(1)
                )
        else:
            keep[r // 2] = y

    for load in loads[1:]:
        load.wait()
    do_chunk(0)
    for r in far:
        for k in arrival:
            along_x[r, k].wait_recv()
            to_core[r, k] = send(rows.at[r, k], rows.at[r + 1, k], id_s[r, k], at_node(1))
    for k in arrival:
        to_core[0, k].wait_recv()
    do_chunk(1)
    for r in far:
        do_chunk(r)
        for k in arrival:
            to_core[r, k].wait_recv()
        do_chunk(r + 1)

    x_sums, z_sums = {}, {}
    for r in far:
        for k in order + [0]:
            core_sums[r, k].wait_recv()
            x_out[r // 2 - 1, k] = (
                keep[r // 2, k] + sib_in[r // 2, k].astype(jnp.float32)
            ).astype(jnp.bfloat16)
            x_sums[r, k] = send(
                x_out.at[r // 2 - 1, k], x_in.at[r // 2 - 1, k], id_rx[r, k], at_node(r)
            )
    for k in order + [0]:
        core_sums[0, k].wait_recv()
        total = keep[0, k] + sib_in[0, k].astype(jnp.float32)
        for r in far:
            x_sums[r, k].wait_recv()
            total = total + x_in[r // 2 - 1, k].astype(jnp.float32)
        if k:
            z_out[k] = total.astype(jnp.bfloat16)
            z_sums[k] = send(z_out.at[k], z_in.at[k], id_rz[k], at_local(k))
    for k in reversed(order):
        z_sums[k].wait_recv()
        total = total + z_in[k].astype(jnp.float32)
    out_ref[...] = total.astype(jnp.bfloat16)

    for copy in started:
        copy.wait_send()


def dense_shards(*args):
    tokens, expert_ids = args[0], args[1]
    tok, width = tokens.shape
    hidden, shared_hidden = args[6].shape[2], args[3].shape[1]
    nodes, locals_ = lax.axis_size("node"), lax.axis_size("local")
    experts = nodes * locals_ // SHARDS
    pairs = nodes // 2
    copies = (locals_ - 1) * 2 + (pairs - 1) * locals_ * 2 + pairs * locals_ * 2
    bf16, f32 = jnp.bfloat16, jnp.float32
    any_spec, vmem_spec = pl.BlockSpec(memory_space=pl.ANY), pl.BlockSpec(memory_space=pltpu.VMEM)
    return pl.pallas_call(
        functools.partial(dense_kernel, (nodes, locals_, width, experts)),
        out_shape=jax.ShapeDtypeStruct((tok, width), bf16),
        in_specs=[any_spec, vmem_spec, vmem_spec] + [any_spec] * 6,
        out_specs=vmem_spec,
        scratch_shapes=[
            pltpu.VMEM((nodes, locals_, tok, width + 128), bf16),
            pltpu.VMEM((width, shared_hidden), bf16),
            pltpu.VMEM((width, shared_hidden), bf16),
            pltpu.VMEM((shared_hidden, width), bf16),
            pltpu.VMEM((width, hidden), bf16),
            pltpu.VMEM((width, hidden), bf16),
            pltpu.VMEM((hidden, width), bf16),
            pltpu.VMEM((pairs, locals_, tok, width), f32),
            pltpu.VMEM((pairs, locals_, tok, width), bf16),
            pltpu.VMEM((pairs, locals_, tok, width), bf16),
            pltpu.VMEM((pairs - 1, locals_, tok, width), bf16),
            pltpu.VMEM((pairs - 1, locals_, tok, width), bf16),
            pltpu.VMEM((locals_, tok, width), bf16),
            pltpu.VMEM((locals_, tok, width), bf16),
            pltpu.SemaphoreType.DMA((7,)),
            pltpu.SemaphoreType.DMA((copies,)),
            pltpu.SemaphoreType.DMA((copies,)),
        ],
        compiler_params=pltpu.CompilerParams(
            collective_id=0, has_side_effects=True, vmem_limit_bytes=60 << 20
        ),
        cost_estimate=pl.CostEstimate(
            flops=6 * tok * nodes * locals_ * width * hidden,
            bytes_accessed=2 * 3 * width * (hidden + shared_hidden),
            transcendentals=0,
        ),
    )(tokens, expert_ids.T, args[2].T, *args[3:])


def shards(*args):
    expert_ids = args[1]
    nodes, locals_ = lax.axis_size("node"), lax.axis_size("local")
    experts = nodes * locals_ // SHARDS
    every_expert = expert_ids.shape[1] == experts and 3 * experts <= 128
    if every_expert and nodes >= 4 and is_power(nodes) and is_power(locals_):
        return dense_shards(*args)
    return sparse_shards(*args)


def solution(mesh):
    return jax.shard_map(
        shards,
        mesh=mesh,
        in_specs=(
            P(("groups", "node", "local"), None),
            P(("groups", "node", "local"), None),
            P(("groups", "node", "local"), None),
            P(None, "local"),
            P(None, "local"),
            P("local", None),
            P(("node", "local"), None, None),
            P(("node", "local"), None, None),
            P(("node", "local"), None, None),
        ),
        out_specs=P(("groups", "node", "local"), None),
        check_vma=False,
    )
```

```python
import functools

import jax
import jax.numpy as jnp
from jax import lax
from jax.experimental import pallas as pl
from jax.experimental.pallas import tpu as pltpu
from jax.sharding import PartitionSpec as P

SHARDS = 4
MESH = pl.DeviceIdType.MESH


def run_block(rows, w_gate, w_up, w_down):
    gate_part = jnp.dot(rows, w_gate, preferred_element_type=jnp.float32)
    up_part = jnp.dot(rows, w_up, preferred_element_type=jnp.float32)
    hidden = (jax.nn.silu(gate_part) * up_part).astype(jnp.bfloat16)
    return jnp.dot(hidden, w_down, preferred_element_type=jnp.float32)


def sparse_shards(
    tokens,
    expert_ids,
    gate_values,
    shared_gate,
    shared_up,
    shared_down,
    expert_gate,
    expert_up,
    expert_down,
):
    tok_dev, model_width = tokens.shape
    top_count = expert_ids.shape[1]
    node_count = lax.axis_size("node")
    local_count = lax.axis_size("local")
    expert_count = node_count * local_count // SHARDS
    capacity = min(tok_dev, max(2, 3 * tok_dev * top_count // (2 * expert_count)))
    shared_terms = run_block(
        lax.all_gather(tokens, "local", axis=0, tiled=True), shared_gate, shared_up, shared_down
    )
    shared_out = lax.psum_scatter(shared_terms, "local", scatter_dimension=0, tiled=True)
    chosen = expert_ids[:, :, None] == jnp.arange(expert_count, dtype=jnp.int32)
    onehot = jnp.any(chosen, axis=1).astype(jnp.float32)
    weight_table = jnp.sum(jnp.where(chosen, gate_values[:, :, None], jnp.float32(0.0)), axis=1)
    position = jnp.cumsum(onehot, axis=0) - onehot
    slot_iota = jnp.arange(capacity).astype(jnp.float32)
    picker = onehot[:, :, None] * (position[:, :, None] == slot_iota).astype(jnp.float32)
    slot_rows = jnp.einsum(
        "tec,td->ecd", picker.astype(jnp.bfloat16), tokens, preferred_element_type=jnp.float32
    ).astype(jnp.bfloat16)
    outgoing = jnp.repeat(slot_rows, SHARDS, axis=0)
    row_block = lax.all_to_all(outgoing, ("node", "local"), split_axis=0, concat_axis=0, tiled=True)
    leading = row_block.shape[:-1]
    flat_rows = row_block.reshape(-1, model_width)
    result = run_block(flat_rows, expert_gate[0], expert_up[0], expert_down[0])
    partial_out = result.astype(jnp.bfloat16).reshape(leading + (model_width,))
    returned = lax.all_to_all(
        partial_out, ("node", "local"), split_axis=0, concat_axis=0, tiled=True
    )
    expert_result = jnp.sum(
        returned.astype(jnp.float32).reshape(expert_count, SHARDS, capacity, model_width), axis=1
    )
    scaled = picker * weight_table[:, :, None]
    routed = jnp.einsum("tec,ecd->td", scaled, expert_result, precision=lax.Precision.HIGHEST)
    return (shared_out + routed).astype(jnp.bfloat16)


def flip(value, bits):
    bit = 1
    while bit <= bits:
        if bits & bit:
            value = value + bit - 2 * bit * ((value // bit) % 2)
        bit *= 2
    return value


def is_power(n):
    return n & (n - 1) == 0


def dense_kernel(
    dims,
    tok_ref, ids_ref, val_ref, sg_ref, su_ref, sd_ref, eg_ref, eu_ref, ed_ref,
    out_ref,
    rows, sg, su, sd, eg, eu, ed,
    shared, keep, sib_out, sib_in, x_out, x_in, z_out, z_in,
    load_sem, send_sem, recv_sem,
):
    nodes, locals_, width, experts = dims
    tok = tok_ref.shape[0]
    node, local = lax.axis_index("node"), lax.axis_index("local")
    evens = range(0, nodes, 2)
    far = range(2, nodes, 2)
    order = list(range(1, locals_))

    count = iter(range(1 << 16))
    id_z = {k: next(count) for k in order}
    id_x = {(r, k): next(count) for r in far for k in range(locals_)}
    id_s = {(r, k): next(count) for r in evens for k in range(locals_)}
    id_rs = {(r, k): next(count) for r in evens for k in range(locals_)}
    id_rx = {(r, k): next(count) for r in far for k in range(locals_)}
    id_rz = {k: next(count) for k in order}

    loads = []
    for i, (src, dst) in enumerate((
        (tok_ref, rows.at[0, 0, :, pl.ds(0, width)]),
        (eg_ref.at[0], eg), (eu_ref.at[0], eu), (ed_ref.at[0], ed),
        (sg_ref, sg), (su_ref, su), (sd_ref, sd),
    )):
        loads.append(pltpu.make_async_copy(src, dst, load_sem.at[i]))
        loads[-1].start()

    def at_local(k):
        return {"local": flip(local, k)}

    def at_node(r):
        return {"node": flip(node, r)}

    partners = [at_local(k) for k in order] + [at_node(r) for r in far] + [at_node(1)]
    barrier = pltpu.get_barrier_semaphore()
    for where in partners:
        pl.semaphore_signal(barrier, inc=1, device_id=where, device_id_type=MESH)

    lane = lax.broadcasted_iota(jnp.int32, (tok, 128), 1)
    lane_expert = lax.rem(lane, experts)
    across = lax.broadcasted_iota(jnp.int32, (tok, tok), 1)
    diagonal = lax.broadcasted_iota(jnp.int32, (tok, tok), 0) == across

    def column(line):
        return jnp.sum(jnp.where(diagonal, line, 0.0), axis=1, keepdims=True)

    lane_expert = lane_expert.astype(jnp.float32)
    weight = jnp.zeros((tok, 128), jnp.float32)
    for k in range(ids_ref.shape[0]):
        name = column(ids_ref[k:k + 1, :].astype(jnp.float32))
        weight = weight + jnp.where(name == lane_expert, column(val_ref[k:k + 1, :]), 0.0)
    high = weight.astype(jnp.bfloat16).astype(jnp.float32)
    middle = (weight - high).astype(jnp.bfloat16).astype(jnp.float32)
    low = weight - high - middle
    terms = jnp.where(
        lane < experts, high,
        jnp.where(lane < 2 * experts, middle, jnp.where(lane < 3 * experts, low, 0.0)),
    )
    rows[0, 0, :, width:width + 128] = terms.astype(jnp.bfloat16)
    loads[0].wait()
    pl.semaphore_wait(barrier, len(partners))

    started = []

    def send(src, dst, number, where):
        copy = pltpu.make_async_remote_copy(
            src_ref=src, dst_ref=dst,
            send_sem=send_sem.at[number], recv_sem=recv_sem.at[number],
            device_id=where, device_id_type=MESH,
        )
        copy.start()
        started.append(copy)
        return copy

    own_expert = (node * locals_ + local) // SHARDS

    def block(x, w_gate, w_up, w_down):
        g = jnp.dot(x, w_gate[...], preferred_element_type=jnp.float32)
        u = jnp.dot(x, w_up[...], preferred_element_type=jnp.float32)
        h = (g / (1.0 + jnp.exp(-g)) * u).astype(jnp.bfloat16)
        return jnp.dot(h, w_down[...], preferred_element_type=jnp.float32)

    along_z, along_x, to_core = {}, {}, {}
    core_sums, x_sums, z_sums = {}, {}, {}

    def gather_z(k):
        along_z[k] = send(rows.at[0, 0], rows.at[k, 0], id_z[k], at_local(k))

    def pass_own(k):
        if k:
            along_z[k].wait_recv()
        for r in far:
            along_x[r, k] = send(rows.at[k, 0], rows.at[k, r], id_x[r, k], at_node(r))
        to_core[0, k] = send(rows.at[k, 0], rows.at[k, 1], id_s[0, k], at_node(1))

    def pass_far(k):
        for r in far:
            along_x[r, k].wait_recv()
            to_core[r, k] = send(rows.at[k, r], rows.at[k, r + 1], id_s[r, k], at_node(1))

    def shared_terms():
        held = jnp.concatenate([rows[k, 0].astype(jnp.float32) for k in range(locals_)], axis=0)
        y = block(held[:, :width].astype(jnp.bfloat16), sg, su, sd)
        shared[...] = y.reshape(locals_, tok, width)

    def compute(k):
        for r in evens:
            to_core[r, k].wait_recv()
        held = rows[k].astype(jnp.float32).reshape(nodes * tok, width + 128)
        x = held[:, :width].astype(jnp.bfloat16)
        tail = held[:, width:]
        lanes = lax.broadcasted_iota(jnp.int32, tail.shape, 1)
        mine = (lax.rem(lanes, experts) == own_expert) & (lanes < 3 * experts)
        factor = jnp.sum(jnp.where(mine, tail, 0.0), axis=1, keepdims=True)
        y = (block(x, eg, eu, ed) * factor).reshape(nodes, tok, width)
        for r in reversed(evens):
            sib_out[k, r // 2] = y[r + 1].astype(jnp.bfloat16)
            core_sums[r, k] = send(
                sib_out.at[k, r // 2], sib_in.at[k, r // 2], id_rs[r, k], at_node(1)
            )
            keep[k, r // 2] = y[r]

    def sum_x(k):
        for r in far:
            core_sums[r, k].wait_recv()
            x_out[k, r // 2 - 1] = (
                keep[k, r // 2] + sib_in[k, r // 2].astype(jnp.float32)
            ).astype(jnp.bfloat16)
            x_sums[r, k] = send(
                x_out.at[k, r // 2 - 1], x_in.at[k, r // 2 - 1], id_rx[r, k], at_node(r)
            )

    def sum_z(k):
        core_sums[0, k].wait_recv()
        total = shared[k] + keep[k, 0] + sib_in[k, 0].astype(jnp.float32)
        for r in far:
            x_sums[r, k].wait_recv()
            total = total + x_in[k, r // 2 - 1].astype(jnp.float32)
        if k:
            z_out[k] = total.astype(jnp.bfloat16)
            z_sums[k] = send(z_out.at[k], z_in.at[k], id_rz[k], at_local(k))
        else:
            shared[k] = total

    for k in order:
        gather_z(k)
    arrival = [0] + order
    count = len(arrival)
    pass_own(0)
    for i in range(1, count):
        pass_own(arrival[i])
        if i <= 1:
            pass_far(arrival[0])
    for load in loads[1:]:
        load.wait()
    for i in range(1, count + 2):
        if i < count:
            pass_far(arrival[i])
        if i <= count:
            compute(arrival[i - 1])
        if 2 <= i:
            if i == count + 1:
                shared_terms()
            sum_x(arrival[i - 2])
    for k in order:
        sum_z(k)
    sum_z(0)
    total = shared[0]
    for k in order:
        z_sums[k].wait_recv()
        total = total + z_in[k].astype(jnp.float32)
    out_ref[...] = total.astype(jnp.bfloat16)

    for copy in started:
        copy.wait_send()


def dense_shards(*args):
    tokens, expert_ids = args[0], args[1]
    tok, width = tokens.shape
    hidden, shared_hidden = args[6].shape[2], args[3].shape[1]
    nodes, locals_ = lax.axis_size("node"), lax.axis_size("local")
    experts = nodes * locals_ // SHARDS
    pairs = nodes // 2
    copies = (locals_ - 1) * 2 + (pairs - 1) * locals_ * 2 + pairs * locals_ * 2
    bf16, f32 = jnp.bfloat16, jnp.float32
    any_spec, vmem_spec = pl.BlockSpec(memory_space=pl.ANY), pl.BlockSpec(memory_space=pltpu.VMEM)
    return pl.pallas_call(
        functools.partial(dense_kernel, (nodes, locals_, width, experts)),
        out_shape=jax.ShapeDtypeStruct((tok, width), bf16),
        in_specs=[any_spec, vmem_spec, vmem_spec] + [any_spec] * 6,
        out_specs=vmem_spec,
        scratch_shapes=[
            pltpu.VMEM((locals_, nodes, tok, width + 128), bf16),
            pltpu.VMEM((width, shared_hidden), bf16),
            pltpu.VMEM((width, shared_hidden), bf16),
            pltpu.VMEM((shared_hidden, width), bf16),
            pltpu.VMEM((width, hidden), bf16),
            pltpu.VMEM((width, hidden), bf16),
            pltpu.VMEM((hidden, width), bf16),
            pltpu.VMEM((locals_, tok, width), f32),
            pltpu.VMEM((locals_, pairs, tok, width), f32),
            pltpu.VMEM((locals_, pairs, tok, width), bf16),
            pltpu.VMEM((locals_, pairs, tok, width), bf16),
            pltpu.VMEM((locals_, pairs - 1, tok, width), bf16),
            pltpu.VMEM((locals_, pairs - 1, tok, width), bf16),
            pltpu.VMEM((locals_, tok, width), bf16),
            pltpu.VMEM((locals_, tok, width), bf16),
            pltpu.SemaphoreType.DMA((7,)),
            pltpu.SemaphoreType.DMA((copies,)),
            pltpu.SemaphoreType.DMA((copies,)),
        ],
        compiler_params=pltpu.CompilerParams(
            collective_id=0, has_side_effects=True, vmem_limit_bytes=60 << 20
        ),
        cost_estimate=pl.CostEstimate(
            flops=6 * tok * nodes * locals_ * width * hidden,
            bytes_accessed=2 * 3 * width * (hidden + shared_hidden),
            transcendentals=0,
        ),
    )(tokens, expert_ids.T, args[2].T, *args[3:])


def shards(*args):
    expert_ids = args[1]
    nodes, locals_ = lax.axis_size("node"), lax.axis_size("local")
    experts = nodes * locals_ // SHARDS
    every_expert = expert_ids.shape[1] == experts and 3 * experts <= 128
    if every_expert and nodes >= 4 and is_power(nodes) and is_power(locals_):
        return dense_shards(*args)
    return sparse_shards(*args)


def solution(mesh):
    return jax.shard_map(
        shards,
        mesh=mesh,
        in_specs=(
            P(("groups", "node", "local"), None),
            P(("groups", "node", "local"), None),
            P(("groups", "node", "local"), None),
            P(None, "local"),
            P(None, "local"),
            P("local", None),
            P(("node", "local"), None, None),
            P(("node", "local"), None, None),
            P(("node", "local"), None, None),
        ),
        out_specs=P(("groups", "node", "local"), None),
        check_vma=False,
    )
```

```python
import functools

import jax
import jax.numpy as jnp
from jax import lax
from jax.experimental import pallas as pl
from jax.experimental.pallas import tpu as pltpu
from jax.sharding import PartitionSpec as P

SHARDS = 4
MESH = pl.DeviceIdType.MESH


def run_block(rows, w_gate, w_up, w_down):
    gate_part = jnp.dot(rows, w_gate, preferred_element_type=jnp.float32)
    up_part = jnp.dot(rows, w_up, preferred_element_type=jnp.float32)
    hidden = (jax.nn.silu(gate_part) * up_part).astype(jnp.bfloat16)
    return jnp.dot(hidden, w_down, preferred_element_type=jnp.float32)


def sparse_shards(
    tokens,
    expert_ids,
    gate_values,
    shared_gate,
    shared_up,
    shared_down,
    expert_gate,
    expert_up,
    expert_down,
):
    tok_dev, model_width = tokens.shape
    top_count = expert_ids.shape[1]
    node_count = lax.axis_size("node")
    local_count = lax.axis_size("local")
    expert_count = node_count * local_count // SHARDS
    capacity = min(tok_dev, max(2, 3 * tok_dev * top_count // (2 * expert_count)))
    shared_terms = run_block(
        lax.all_gather(tokens, "local", axis=0, tiled=True), shared_gate, shared_up, shared_down
    )
    shared_out = lax.psum_scatter(shared_terms, "local", scatter_dimension=0, tiled=True)
    chosen = expert_ids[:, :, None] == jnp.arange(expert_count, dtype=jnp.int32)
    onehot = jnp.any(chosen, axis=1).astype(jnp.float32)
    weight_table = jnp.sum(jnp.where(chosen, gate_values[:, :, None], jnp.float32(0.0)), axis=1)
    position = jnp.cumsum(onehot, axis=0) - onehot
    slot_iota = jnp.arange(capacity).astype(jnp.float32)
    picker = onehot[:, :, None] * (position[:, :, None] == slot_iota).astype(jnp.float32)
    slot_rows = jnp.einsum(
        "tec,td->ecd", picker.astype(jnp.bfloat16), tokens, preferred_element_type=jnp.float32
    ).astype(jnp.bfloat16)
    outgoing = jnp.repeat(slot_rows, SHARDS, axis=0)
    row_block = lax.all_to_all(outgoing, ("node", "local"), split_axis=0, concat_axis=0, tiled=True)
    leading = row_block.shape[:-1]
    flat_rows = row_block.reshape(-1, model_width)
    result = run_block(flat_rows, expert_gate[0], expert_up[0], expert_down[0])
    partial_out = result.astype(jnp.bfloat16).reshape(leading + (model_width,))
    returned = lax.all_to_all(
        partial_out, ("node", "local"), split_axis=0, concat_axis=0, tiled=True
    )
    expert_result = jnp.sum(
        returned.astype(jnp.float32).reshape(expert_count, SHARDS, capacity, model_width), axis=1
    )
    scaled = picker * weight_table[:, :, None]
    routed = jnp.einsum("tec,ecd->td", scaled, expert_result, precision=lax.Precision.HIGHEST)
    return (shared_out + routed).astype(jnp.bfloat16)


def flip(value, bits):
    bit = 1
    while bit <= bits:
        if bits & bit:
            value = value + bit - 2 * bit * ((value // bit) % 2)
        bit *= 2
    return value


def is_power(n):
    return n & (n - 1) == 0


def dense_kernel(
    dims,
    tok_ref, ids_ref, val_ref, sg_ref, su_ref, sd_ref, eg_ref, eu_ref, ed_ref,
    out_ref,
    rows, sg, su, sd, eg, eu, ed,
    shared, keep, sib_out, sib_in, x_out, x_in, z_out, z_in,
    load_sem, send_sem, recv_sem,
):
    nodes, locals_, width, experts = dims
    tok = tok_ref.shape[0]
    node, local = lax.axis_index("node"), lax.axis_index("local")
    evens = range(0, nodes, 2)
    far = range(2, nodes, 2)
    order = list(range(1, locals_))

    count = iter(range(1 << 16))
    id_z = {k: next(count) for k in order}
    id_x = {(r, k): next(count) for r in far for k in range(locals_)}
    id_s = {(r, k): next(count) for r in evens for k in range(locals_)}
    id_rs = {(r, k): next(count) for r in evens for k in range(locals_)}
    id_rx = {(r, k): next(count) for r in far for k in range(locals_)}
    id_rz = {k: next(count) for k in order}

    loads = []
    for i, (src, dst) in enumerate((
        (tok_ref, rows.at[0, 0, :, pl.ds(0, width)]),
        (eg_ref.at[0], eg), (eu_ref.at[0], eu), (ed_ref.at[0], ed),
        (sg_ref, sg), (su_ref, su), (sd_ref, sd),
    )):
        loads.append(pltpu.make_async_copy(src, dst, load_sem.at[i]))
        loads[-1].start()

    def at_local(k):
        return {"local": flip(local, k)}

    def at_node(r):
        return {"node": flip(node, r)}

    partners = [at_local(k) for k in order] + [at_node(r) for r in far] + [at_node(1)]
    barrier = pltpu.get_barrier_semaphore()
    for where in partners:
        pl.semaphore_signal(barrier, inc=1, device_id=where, device_id_type=MESH)

    lane = lax.broadcasted_iota(jnp.int32, (tok, 128), 1)
    lane_expert = lax.rem(lane, experts)
    across = lax.broadcasted_iota(jnp.int32, (tok, tok), 1)
    diagonal = lax.broadcasted_iota(jnp.int32, (tok, tok), 0) == across

    def column(line):
        return jnp.sum(jnp.where(diagonal, line, 0.0), axis=1, keepdims=True)

    lane_expert = lane_expert.astype(jnp.float32)
    weight = jnp.zeros((tok, 128), jnp.float32)
    for k in range(ids_ref.shape[0]):
        name = column(ids_ref[k:k + 1, :].astype(jnp.float32))
        weight = weight + jnp.where(name == lane_expert, column(val_ref[k:k + 1, :]), 0.0)
    high = weight.astype(jnp.bfloat16).astype(jnp.float32)
    middle = (weight - high).astype(jnp.bfloat16).astype(jnp.float32)
    low = weight - high - middle
    terms = jnp.where(
        lane < experts, high,
        jnp.where(lane < 2 * experts, middle, jnp.where(lane < 3 * experts, low, 0.0)),
    )
    rows[0, 0, :, width:width + 128] = terms.astype(jnp.bfloat16)
    loads[0].wait()
    pl.semaphore_wait(barrier, len(partners))

    started = []

    def send(src, dst, number, where):
        copy = pltpu.make_async_remote_copy(
            src_ref=src, dst_ref=dst,
            send_sem=send_sem.at[number], recv_sem=recv_sem.at[number],
            device_id=where, device_id_type=MESH,
        )
        copy.start()
        started.append(copy)
        return copy

    own_expert = (node * locals_ + local) // SHARDS

    def block(x, w_gate, w_up, w_down):
        g = jnp.dot(x, w_gate[...], preferred_element_type=jnp.float32)
        u = jnp.dot(x, w_up[...], preferred_element_type=jnp.float32)
        h = (g / (1.0 + jnp.exp(-g)) * u).astype(jnp.bfloat16)
        return jnp.dot(h, w_down[...], preferred_element_type=jnp.float32)

    along_z, along_x, to_core = {}, {}, {}
    core_sums, x_sums, z_sums = {}, {}, {}

    def gather_z(k):
        along_z[k] = send(rows.at[0, 0], rows.at[k, 0], id_z[k], at_local(k))

    def pass_own(k):
        if k:
            along_z[k].wait_recv()
        for r in far:
            along_x[r, k] = send(rows.at[k, 0], rows.at[k, r], id_x[r, k], at_node(r))
        to_core[0, k] = send(rows.at[k, 0], rows.at[k, 1], id_s[0, k], at_node(1))

    def pass_far(k):
        for r in far:
            along_x[r, k].wait_recv()
            to_core[r, k] = send(rows.at[k, r], rows.at[k, r + 1], id_s[r, k], at_node(1))

    def shared_terms():
        held = jnp.concatenate([rows[k, 0].astype(jnp.float32) for k in range(locals_)], axis=0)
        y = block(held[:, :width].astype(jnp.bfloat16), sg, su, sd)
        shared[...] = y.reshape(locals_, tok, width)

    def compute(k):
        for r in evens:
            to_core[r, k].wait_recv()
        held = rows[k].astype(jnp.float32).reshape(nodes * tok, width + 128)
        x = held[:, :width].astype(jnp.bfloat16)
        tail = held[:, width:]
        lanes = lax.broadcasted_iota(jnp.int32, tail.shape, 1)
        mine = (lax.rem(lanes, experts) == own_expert) & (lanes < 3 * experts)
        factor = jnp.sum(jnp.where(mine, tail, 0.0), axis=1, keepdims=True)
        y = (block(x, eg, eu, ed) * factor).reshape(nodes, tok, width)
        for r in reversed(evens):
            sib_out[k, r // 2] = y[r + 1].astype(jnp.bfloat16)
            core_sums[r, k] = send(
                sib_out.at[k, r // 2], sib_in.at[k, r // 2], id_rs[r, k], at_node(1)
            )
            keep[k, r // 2] = y[r]

    def sum_x(k):
        for r in far:
            core_sums[r, k].wait_recv()
            x_out[k, r // 2 - 1] = (
                keep[k, r // 2] + sib_in[k, r // 2].astype(jnp.float32)
            ).astype(jnp.bfloat16)
            x_sums[r, k] = send(
                x_out.at[k, r // 2 - 1], x_in.at[k, r // 2 - 1], id_rx[r, k], at_node(r)
            )

    def sum_z(k):
        core_sums[0, k].wait_recv()
        total = shared[k] + keep[k, 0] + sib_in[k, 0].astype(jnp.float32)
        for r in far:
            x_sums[r, k].wait_recv()
            total = total + x_in[k, r // 2 - 1].astype(jnp.float32)
        if k:
            z_out[k] = total.astype(jnp.bfloat16)
            z_sums[k] = send(z_out.at[k], z_in.at[k], id_rz[k], at_local(k))
        else:
            shared[k] = total

    for k in order:
        gather_z(k)
    arrival = [0] + order
    count = len(arrival)
    pass_own(0)
    for i in range(1, count):
        pass_own(arrival[i])
        if i <= 1:
            pass_far(arrival[0])
    for load in loads[1:]:
        load.wait()
    for i in range(1, count + 2):
        if i < count:
            pass_far(arrival[i])
        if i <= count:
            compute(arrival[i - 1])
        if 2 <= i:
            sum_x(arrival[i - 2])
    shared_terms()
    for k in order:
        sum_z(k)
    sum_z(0)
    total = shared[0]
    for k in order:
        z_sums[k].wait_recv()
        total = total + z_in[k].astype(jnp.float32)
    out_ref[...] = total.astype(jnp.bfloat16)

    for copy in started:
        copy.wait_send()


def dense_shards(*args):
    tokens, expert_ids = args[0], args[1]
    tok, width = tokens.shape
    hidden, shared_hidden = args[6].shape[2], args[3].shape[1]
    nodes, locals_ = lax.axis_size("node"), lax.axis_size("local")
    experts = nodes * locals_ // SHARDS
    pairs = nodes // 2
    copies = (locals_ - 1) * 2 + (pairs - 1) * locals_ * 2 + pairs * locals_ * 2
    bf16, f32 = jnp.bfloat16, jnp.float32
    any_spec, vmem_spec = pl.BlockSpec(memory_space=pl.ANY), pl.BlockSpec(memory_space=pltpu.VMEM)
    return pl.pallas_call(
        functools.partial(dense_kernel, (nodes, locals_, width, experts)),
        out_shape=jax.ShapeDtypeStruct((tok, width), bf16),
        in_specs=[any_spec, vmem_spec, vmem_spec] + [any_spec] * 6,
        out_specs=vmem_spec,
        scratch_shapes=[
            pltpu.VMEM((locals_, nodes, tok, width + 128), bf16),
            pltpu.VMEM((width, shared_hidden), bf16),
            pltpu.VMEM((width, shared_hidden), bf16),
            pltpu.VMEM((shared_hidden, width), bf16),
            pltpu.VMEM((width, hidden), bf16),
            pltpu.VMEM((width, hidden), bf16),
            pltpu.VMEM((hidden, width), bf16),
            pltpu.VMEM((locals_, tok, width), f32),
            pltpu.VMEM((locals_, pairs, tok, width), f32),
            pltpu.VMEM((locals_, pairs, tok, width), bf16),
            pltpu.VMEM((locals_, pairs, tok, width), bf16),
            pltpu.VMEM((locals_, pairs - 1, tok, width), bf16),
            pltpu.VMEM((locals_, pairs - 1, tok, width), bf16),
            pltpu.VMEM((locals_, tok, width), bf16),
            pltpu.VMEM((locals_, tok, width), bf16),
            pltpu.SemaphoreType.DMA((7,)),
            pltpu.SemaphoreType.DMA((copies,)),
            pltpu.SemaphoreType.DMA((copies,)),
        ],
        compiler_params=pltpu.CompilerParams(
            collective_id=0, has_side_effects=True, vmem_limit_bytes=60 << 20
        ),
        cost_estimate=pl.CostEstimate(
            flops=6 * tok * nodes * locals_ * width * hidden,
            bytes_accessed=2 * 3 * width * (hidden + shared_hidden),
            transcendentals=0,
        ),
    )(tokens, expert_ids.T, args[2].T, *args[3:])


def shards(*args):
    expert_ids = args[1]
    nodes, locals_ = lax.axis_size("node"), lax.axis_size("local")
    experts = nodes * locals_ // SHARDS
    every_expert = expert_ids.shape[1] == experts and 3 * experts <= 128
    if every_expert and nodes >= 4 and is_power(nodes) and is_power(locals_):
        return dense_shards(*args)
    return sparse_shards(*args)


def solution(mesh):
    return jax.shard_map(
        shards,
        mesh=mesh,
        in_specs=(
            P(("groups", "node", "local"), None),
            P(("groups", "node", "local"), None),
            P(("groups", "node", "local"), None),
            P(None, "local"),
            P(None, "local"),
            P("local", None),
            P(("node", "local"), None, None),
            P(("node", "local"), None, None),
            P(("node", "local"), None, None),
        ),
        out_specs=P(("groups", "node", "local"), None),
        check_vma=False,
    )
```
